32 devices in a mesh: row: 8 (over z, x), col: 4 (over y, core).
Axes of the slice: x: 2, y: 2, z: 4, core: 2. Of those that a mesh axis runs over, the one named last changes fastest.
Arguments:
- records: bfloat16 [128, 8, 1500], P('row', 'col'), may hold values from -6 to 6
- channel_live: int32 [128], replicated, may hold values 0 or 1
- minute_valid: int32 [8], replicated, may hold values 0 or 1
Outputs:
- correlations: bfloat16 [128, 128, 801], P('row', 'col')
The draws below stay inside these ranges and needn't reach their ends.
All inputs are finite; a program needn't handle non-finite values.
Results may differ from the reference program's by a relative error of at most 0.0075.
Values may be sent and summed in bfloat16 or wider, within the bound.
A program may use at most 64 MiB of HBM per device.

```python
import math
import jax
import jax.numpy as jnp
from jax import lax

SEG = 1500
F = 640
BAND = 32
MAXLAG = 400
NCH = 128
MINUTES = 8


def plant(drawn, key, smallest, high):
    extent = drawn.shape
    place = [jax.random.randint(jax.random.fold_in(key, axis), (), 0, extent[axis]) for axis in range(len(extent))]
    drawn = drawn.at[tuple(place)].set(smallest)
    longest = extent.index(max(extent))
    place[longest] = (place[longest] + 1) % extent[longest]
    return drawn.at[tuple(place)].set(high)


def steps_of(rng, shape, split, least, largest):
    factor_of = 1.0
    for axis_at, blocks in split:
        steps = jax.random.uniform(jax.random.fold_in(jax.random.fold_in(rng, 6), axis_at), (blocks,), jnp.float32, least / len(split), largest / len(split))
        factor_of = factor_of * jnp.repeat(jnp.exp(steps), shape[axis_at] // blocks).reshape((-1,) + (1,) * (len(shape) - 1 - axis_at))
    return factor_of


def noise(own_key, extent, spread, most, split=(), kind=jnp.bfloat16):
    values = spread * jax.random.normal(own_key, extent, jnp.float32)
    if split:
        values = values * steps_of(own_key, extent, split, -0.22, 0.18)
    return jnp.clip(values, -most, most).astype(kind)


def setup_inputs(seed: int = 0) -> dict:
    splits = jax.random.split(jax.random.key(seed), 4)
    records = noise(splits[0], (NCH, MINUTES, SEG), 1.0, 6.0, ((0, 8), (1, 4)))
    channel_live = plant((jax.random.randint(splits[1], (NCH,), 0, 8) < 7).astype(jnp.int32), jax.random.fold_in(splits[1], 1), 0, 1)
    minute_valid = plant((jax.random.randint(splits[2], (MINUTES,), 0, 4) < 3).astype(jnp.int32), jax.random.fold_in(splits[2], 1), 0, 1)
    return {"records": records, "channel_live": channel_live, "minute_valid": minute_valid}


def forward_table(length, nfreq):
    times = jnp.arange(length, dtype=jnp.int32)[:, None]
    freqs = jnp.arange(1, nfreq + 1, dtype=jnp.int32)[None, :]
    phase = (times * freqs % length).astype(jnp.float32) * jnp.float32(2.0 * math.pi / length)
    return jnp.concatenate([jnp.cos(phase), -jnp.sin(phase)], axis=1).astype(jnp.bfloat16)

def inverse_table(length, nfreq, maxlag):
    freqs = jnp.arange(1, nfreq + 1, dtype=jnp.int32)[:, None]
    shifts = jnp.arange(-maxlag, maxlag + 1, dtype=jnp.int32)[None, :]
    phase = jnp.mod(freqs * shifts, length).astype(jnp.float32) * jnp.float32(2.0 * math.pi / length)
    return jnp.concatenate([jnp.cos(phase), -jnp.sin(phase)], axis=0).astype(jnp.bfloat16)

def whiten(signal, live, valid, table, band):
    chans, mins, length = signal.shape
    nfreq = table.shape[1] // 2
    spectrum = jnp.dot(signal.reshape(chans * mins, length), table, preferred_element_type=jnp.float32)
    grouped = spectrum.reshape(chans, mins, 2, nfreq // band, band)
    power = lax.optimization_barrier(jnp.mean(grouped * grouped, axis=(2, 4)))
    weight = lax.rsqrt(power + 1e-06) * live.astype(jnp.float32)[:, None, None] * valid.astype(jnp.float32)[None, :, None]
    return (grouped * weight[:, :, None, :, None]).reshape(chans, mins, 2 * nfreq).astype(jnp.bfloat16)

def correlate(rows, cols, itab, count):
    nfreq = rows.shape[2] // 2
    row_real = rows[:, :, :nfreq].astype(jnp.float32)
    row_imag = rows[:, :, nfreq:].astype(jnp.float32)
    col_real = cols[:, :, :nfreq].astype(jnp.float32)
    col_imag = cols[:, :, nfreq:].astype(jnp.float32)
    high = lax.Precision.HIGHEST
    real_sum = jnp.einsum('imf,jmf->ijf', row_real, col_real, precision=high) + jnp.einsum('imf,jmf->ijf', row_imag, col_imag, precision=high)
    imag_sum = jnp.einsum('imf,jmf->ijf', row_imag, col_real, precision=high) - jnp.einsum('imf,jmf->ijf', row_real, col_imag, precision=high)
    stacked = (jnp.concatenate([real_sum, imag_sum], axis=-1) / jnp.float32(count)).astype(jnp.bfloat16)
    lagged = jnp.dot(stacked.reshape(-1, 2 * nfreq), itab, preferred_element_type=jnp.float32)
    lagged = lagged * jnp.float32(1.0 / math.sqrt(nfreq))
    return lagged.astype(jnp.bfloat16).reshape(rows.shape[0], cols.shape[0], itab.shape[1])

def reference(records, channel_live, minute_valid):
    table = forward_table(SEG, F)
    spectra = whiten(records, channel_live, minute_valid, table, BAND)
    itab = inverse_table(SEG, F, MAXLAG)
    block = math.gcd(NCH, 32)
    grouped = spectra.reshape(NCH // block, block, MINUTES, 2 * F)

    def one_block(rows):
        return correlate(rows, spectra, itab, MINUTES)
    result = lax.map(one_block, grouped)
    return result.reshape(NCH, NCH, 2 * MAXLAG + 1)
```

```python
import functools
import math

import jax
import jax.numpy as jnp
import numpy as np
from jax import lax
from jax.experimental import pallas as pl
from jax.experimental.pallas import tpu as pltpu
from jax.sharding import PartitionSpec as P

F = 640
BAND = 32
MAXLAG = 400
LANES = 128
MESH = pl.DeviceIdType.MESH


def forward_table(length, nfreq, padded):
    times = np.arange(length, dtype=np.int64)[:, None]
    freqs = np.arange(1, nfreq + 1, dtype=np.int64)[None, :]
    phase = (times * freqs % length).astype(np.float32) * np.float32(2.0 * math.pi / length)
    table = np.concatenate([np.cos(phase), -np.sin(phase)], axis=1)
    return np.pad(table, ((0, padded - length), (0, 0))).astype(jnp.bfloat16)


def inverse_table(length, nfreq, maxlag, padded):
    freqs = np.arange(1, nfreq + 1, dtype=np.int64)[:, None]
    shifts = np.arange(-maxlag, maxlag + 1, dtype=np.int64)[None, :]
    phase = np.mod(freqs * shifts, length).astype(np.float32) * np.float32(2.0 * math.pi / length)
    table = np.concatenate([np.cos(phase), -np.sin(phase)], axis=0)
    return np.pad(table, ((0, 0), (0, padded - table.shape[1]))).astype(jnp.bfloat16)


def kernel(
    rows_n, cols_n, rc, pm,
    rec_ref, ftab_hbm, itab_hbm, out_ref,
    ftab, itab, spec, rowb, colb, rowf, colf, stacked,
    tab_sem, z_send, z_recv, r_send, r_recv, c_send, c_recv,
):
    k = rows_n // cols_n
    me_r = lax.axis_index("row")
    me_c = lax.axis_index("col")
    me_q = me_r // k
    me_s = lax.rem(me_r, k)
    minutes = pm * cols_n
    jc = k * rc

    f_copy = pltpu.make_async_copy(ftab_hbm, ftab, tab_sem.at[0])
    i_copy = pltpu.make_async_copy(itab_hbm, itab, tab_sem.at[1])
    f_copy.start()
    i_copy.start()

    barrier = pltpu.get_barrier_semaphore()
    peers = []
    for d in range(1, cols_n):
        peers.append((lax.rem(me_q + d, cols_n) * k + me_s, me_c))
    for e in range(k):
        for d in range(cols_n):
            if e or d:
                peers.append((me_q * k + lax.rem(me_s + e, k), lax.rem(me_c + d, cols_n)))
    for peer in peers:
        pl.semaphore_signal(barrier, inc=1, device_id=peer, device_id_type=MESH)

    f_copy.wait()
    raw = jnp.dot(rec_ref[...], ftab[...], preferred_element_type=jnp.float32)
    re = raw[:, :F]
    im = raw[:, F:]
    sq = re * re + im * im
    nv = F // LANES
    n = pm * rc
    sq = jnp.concatenate([sq[:, v * LANES:(v + 1) * LANES] for v in range(nv)], axis=0)
    shift = int(math.log2(BAND))
    same = (lax.broadcasted_iota(jnp.int32, (LANES, LANES), 0) >> shift) == (
        lax.broadcasted_iota(jnp.int32, (LANES, LANES), 1) >> shift
    )
    ones = jnp.where(same, 1.0, 0.0).astype(jnp.bfloat16)
    hi = sq.astype(jnp.bfloat16)
    rest = sq - hi.astype(jnp.float32)
    mid = rest.astype(jnp.bfloat16)
    low = (rest - mid.astype(jnp.float32)).astype(jnp.bfloat16)
    power = (
        jnp.dot(hi, ones, preferred_element_type=jnp.float32)
        + jnp.dot(mid, ones, preferred_element_type=jnp.float32)
        + jnp.dot(low, ones, preferred_element_type=jnp.float32)
    ) * jnp.float32(1.0 / (2 * BAND))
    weight = lax.rsqrt(power + 1e-06)
    weight = jnp.concatenate([weight[v * n:(v + 1) * n] for v in range(nv)], axis=1)
    white_re = (re * weight).astype(jnp.bfloat16)
    white_im = (im * weight).astype(jnp.bfloat16)
    for m in range(pm):
        spec[me_q, m, :, :F] = white_re[m * rc:(m + 1) * rc]
        spec[me_q, m, :, F:] = white_im[m * rc:(m + 1) * rc]

    pl.semaphore_wait(barrier, len(peers))

    sends = []
    for d in range(1, cols_n):
        to_q = lax.rem(me_q + d, cols_n)
        copy = pltpu.make_async_remote_copy(
            spec.at[me_q], spec.at[me_q], z_send.at[d], z_recv.at[me_q],
            device_id=(to_q * k + me_s, me_c), device_id_type=MESH,
        )
        copy.start()
        sends.append(copy)
    for d in range(1, cols_n):
        to_c = lax.rem(me_c + d, cols_n)
        copy = pltpu.make_async_remote_copy(
            spec.at[me_q], rowb.at[me_c], r_send.at[d], r_recv.at[me_c],
            device_id=(me_r, to_c), device_id_type=MESH,
        )
        copy.start()
        sends.append(copy)
    rowb[me_c] = spec[me_q]
    guarded = []
    for d in range(cols_n):
        q = lax.rem(me_q + d, cols_n)
        if d:
            pltpu.make_async_remote_copy(
                spec.at[q], spec.at[q], z_send.at[d], z_recv.at[q],
                device_id=(q * k + me_s, me_c), device_id_type=MESH,
            ).wait_recv()
        for e in range(k):
            copy = pltpu.make_async_remote_copy(
                spec.at[q], colb.at[me_s, me_c], c_send.at[d, e], c_recv.at[me_s, me_c],
                device_id=(me_q * k + lax.rem(me_s + e, k), q), device_id_type=MESH,
            )
            if e:
                copy.start()
                sends.append(copy)
            else:
                @pl.when(q != me_c)
                def _():
                    copy.start()

                @pl.when(q == me_c)
                def _():
                    colb[me_s, me_c] = spec[q]
                guarded.append((q, copy))

    for d in range(cols_n):
        c = lax.rem(me_c + d, cols_n)
        if d:
            pltpu.make_async_remote_copy(
                spec.at[me_q], rowb.at[c], r_send.at[d], r_recv.at[c],
                device_id=(me_r, c), device_id_type=MESH,
            ).wait_recv()
        for m in range(pm):
            rowf[:, d * pm + m, :] = rowb[c, m].astype(jnp.float32)
    for e in range(k):
        s = lax.rem(me_s + e, k)
        for d in range(cols_n):
            c = lax.rem(me_c + d, cols_n)
            if e or d:
                pltpu.make_async_remote_copy(
                    spec.at[me_q], colb.at[s, c], c_send.at[d, e], c_recv.at[s, c],
                    device_id=(me_q * k + s, c), device_id_type=MESH,
                ).wait_recv()
            for m in range(pm):
                colf[d * pm + m, pl.ds(pl.multiple_of(s * rc, rc), rc), :] = (
                    colb[s, c, m].astype(jnp.float32)
                )

    i_copy.wait()
    scale = jnp.float32(1.0 / minutes)
    step = 2

    def pair(p, carry):
        for v in range(nv):
            lo = v * LANES
            hi_ = F + v * LANES
            acc = [[None, None] for _ in range(step)]
            for m in range(minutes):
                cr = colf[m, :, lo:lo + LANES]
                ci = colf[m, :, hi_:hi_ + LANES]
                for u in range(step):
                    rr = rowf[p * step + u, m:m + 1, lo:lo + LANES]
                    ri = rowf[p * step + u, m:m + 1, hi_:hi_ + LANES]
                    real = rr * cr + ri * ci
                    imag = ri * cr - rr * ci
                    acc[u][0] = real if m == 0 else acc[u][0] + real
                    acc[u][1] = imag if m == 0 else acc[u][1] + imag
            for u in range(step):
                stacked[p * step + u, :, lo:lo + LANES] = (acc[u][0] * scale).astype(jnp.bfloat16)
                stacked[p * step + u, :, hi_:hi_ + LANES] = (acc[u][1] * scale).astype(jnp.bfloat16)
        return carry

    lax.fori_loop(0, rc // step, pair, 0)

    group = 256 // jc
    lags = out_ref.shape[2]

    def lagged(b, carry):
        left = stacked[pl.ds(b * group, group)].reshape(group * jc, 2 * F)
        result = jnp.dot(left, itab[...], preferred_element_type=jnp.float32)
        result = (result * jnp.float32(1.0 / math.sqrt(F))).astype(jnp.bfloat16)
        out_ref[pl.ds(b * group, group)] = result[:, :lags].reshape(group, jc, lags)
        return carry

    lax.fori_loop(0, rc // group, lagged, 0)

    for copy in sends:
        copy.wait_send()
    for q, copy in guarded:
        @pl.when(q != me_c)
        def _():
            copy.wait_send()


def body(rows_n, cols_n, records, channel_live, minute_valid):
    rc, pm, length = records.shape
    padded = -(-length // 256) * 256
    lags = 2 * MAXLAG + 1
    lag_pad = -(-lags // LANES) * LANES
    k = rows_n // cols_n
    minutes = pm * cols_n
    live = lax.dynamic_slice_in_dim(channel_live, lax.axis_index("row") * rc, rc)
    valid = lax.dynamic_slice_in_dim(minute_valid, lax.axis_index("col") * pm, pm)
    keep = (live[:, None] * valid[None, :]).astype(jnp.bfloat16)
    rec = (records * keep[:, :, None]).transpose(1, 0, 2)
    rec = jnp.pad(rec, ((0, 0), (0, 0), (0, padded - length))).reshape(pm * rc, padded)
    ftab = jnp.asarray(forward_table(length, F, padded))
    itab = jnp.asarray(inverse_table(length, F, MAXLAG, lag_pad))
    jc = k * rc
    return pl.pallas_call(
        functools.partial(kernel, rows_n, cols_n, rc, pm),
        out_shape=jax.ShapeDtypeStruct((rc, jc, lags), jnp.bfloat16),
        in_specs=[
            pl.BlockSpec(memory_space=pltpu.VMEM),
            pl.BlockSpec(memory_space=pl.ANY),
            pl.BlockSpec(memory_space=pl.ANY),
        ],
        out_specs=pl.BlockSpec(memory_space=pltpu.VMEM),
        scratch_shapes=[
            pltpu.VMEM((padded, 2 * F), jnp.bfloat16),
            pltpu.VMEM((2 * F, lag_pad), jnp.bfloat16),
            pltpu.VMEM((cols_n, pm, rc, 2 * F), jnp.bfloat16),
            pltpu.VMEM((cols_n, pm, rc, 2 * F), jnp.bfloat16),
            pltpu.VMEM((k, cols_n, pm, rc, 2 * F), jnp.bfloat16),
            pltpu.VMEM((rc, minutes, 2 * F), jnp.float32),
            pltpu.VMEM((minutes, jc, 2 * F), jnp.float32),
            pltpu.VMEM((rc, jc, 2 * F), jnp.bfloat16),
            pltpu.SemaphoreType.DMA((2,)),
            pltpu.SemaphoreType.DMA((cols_n,)),
            pltpu.SemaphoreType.DMA((cols_n,)),
            pltpu.SemaphoreType.DMA((cols_n,)),
            pltpu.SemaphoreType.DMA((cols_n,)),
            pltpu.SemaphoreType.DMA((cols_n, k)),
            pltpu.SemaphoreType.DMA((k, cols_n)),
        ],
        compiler_params=pltpu.CompilerParams(
            collective_id=0, has_side_effects=True, vmem_limit_bytes=56 * 1024 * 1024
        ),
    )(rec, ftab, itab)


def solution(mesh):
    in_specs = (P("row", "col", None), P(), P())
    out_specs = P("row", "col", None)
    run = functools.partial(body, mesh.shape["row"], mesh.shape["col"])
    return jax.shard_map(run, mesh=mesh, in_specs=in_specs, out_specs=out_specs, check_vma=False)
```

```python
import functools
import math

import jax
import jax.numpy as jnp
import numpy as np
from jax import lax
from jax.experimental import pallas as pl
from jax.experimental.pallas import tpu as pltpu
from jax.sharding import PartitionSpec as P

F = 640
BAND = 32
MAXLAG = 400
LANES = 128
MESH = pl.DeviceIdType.MESH


def forward_table(length, nfreq, padded):
    times = np.arange(length, dtype=np.int64)[:, None]
    freqs = np.arange(1, nfreq + 1, dtype=np.int64)[None, :]
    phase = (times * freqs % length).astype(np.float32) * np.float32(2.0 * math.pi / length)
    table = np.concatenate([np.cos(phase), -np.sin(phase)], axis=1)
    return np.pad(table, ((0, padded - length), (0, 0))).astype(jnp.bfloat16)


def inverse_table(length, nfreq, maxlag, padded):
    freqs = np.arange(1, nfreq + 1, dtype=np.int64)[:, None]
    shifts = np.arange(-maxlag, maxlag + 1, dtype=np.int64)[None, :]
    phase = np.mod(freqs * shifts, length).astype(np.float32) * np.float32(2.0 * math.pi / length)
    table = np.concatenate([np.cos(phase), -np.sin(phase)], axis=0)
    return np.pad(table, ((0, 0), (0, padded - table.shape[1]))).astype(jnp.bfloat16)


def kernel(
    rows_n, cols_n, rc, pm,
    live_ref, valid_ref, rec_ref, ftab_hbm, itab_hbm, out_ref,
    ftab, itab, spec, rowb, colb, rowf, colf, stacked, white,
    tab_sem, z_send, z_recv, r_send, r_recv, c_send, c_recv,
):
    k = rows_n // cols_n
    me_r = lax.axis_index("row")
    me_c = lax.axis_index("col")
    me_q = me_r // k
    me_s = lax.rem(me_r, k)
    minutes = pm * cols_n
    jc = k * rc

    f_copy = pltpu.make_async_copy(ftab_hbm, ftab, tab_sem.at[0])
    i_copy = pltpu.make_async_copy(itab_hbm, itab, tab_sem.at[1])
    f_copy.start()
    i_copy.start()

    barrier = pltpu.get_barrier_semaphore()
    peers = []
    for d in range(1, cols_n):
        peers.append((lax.rem(me_q + d, cols_n) * k + me_s, me_c))
    for e in range(k):
        for d in range(cols_n):
            if e or d:
                peers.append((me_q * k + lax.rem(me_s + e, k), lax.rem(me_c + d, cols_n)))
    for peer in peers:
        pl.semaphore_signal(barrier, inc=1, device_id=peer, device_id_type=MESH)

    f_copy.wait()
    raw = jnp.dot(rec_ref[...].reshape(pm * rc, rec_ref.shape[2]), ftab[...], preferred_element_type=jnp.float32)
    re = raw[:, :F]
    im = raw[:, F:]
    sq = re * re + im * im
    nv = F // LANES
    n = pm * rc
    sq = jnp.concatenate([sq[:, v * LANES:(v + 1) * LANES] for v in range(nv)], axis=0)
    shift = int(math.log2(BAND))
    same = (lax.broadcasted_iota(jnp.int32, (LANES, LANES), 0) >> shift) == (
        lax.broadcasted_iota(jnp.int32, (LANES, LANES), 1) >> shift
    )
    ones = jnp.where(same, 1.0, 0.0).astype(jnp.bfloat16)
    hi = sq.astype(jnp.bfloat16)
    rest = sq - hi.astype(jnp.float32)
    mid = rest.astype(jnp.bfloat16)
    low = (rest - mid.astype(jnp.float32)).astype(jnp.bfloat16)
    power = (
        jnp.dot(hi, ones, preferred_element_type=jnp.float32)
        + jnp.dot(mid, ones, preferred_element_type=jnp.float32)
        + jnp.dot(low, ones, preferred_element_type=jnp.float32)
    ) * jnp.float32(1.0 / (2 * BAND))
    weight = lax.rsqrt(power + 1e-06)
    weight = jnp.concatenate([weight[v * n:(v + 1) * n] for v in range(nv)], axis=1)
    row_at = lax.broadcasted_iota(jnp.int32, (rc, 1), 0)
    live = jnp.zeros((rc, 1), jnp.int32)
    for i in range(rc):
        live = jnp.where(row_at == i, live_ref[me_r * rc + i], live)
    live = live.astype(jnp.float32)
    for v in range(nv):
        at = slice(v * LANES, (v + 1) * LANES)
        white[v] = re[:, at] * weight[:, at]
        white[nv + v] = im[:, at] * weight[:, at]
    for m in range(pm):
        keep = live * valid_ref[me_c * pm + m].astype(jnp.float32)
        for v in range(2 * nv):
            spec[me_q, m, :, v * LANES:(v + 1) * LANES] = (
                white[v, pl.ds(m, rc, stride=pm), :] * keep
            ).astype(jnp.bfloat16)

    pl.semaphore_wait(barrier, len(peers))

    sends = []
    for d in range(1, cols_n):
        to_q = lax.rem(me_q + d, cols_n)
        copy = pltpu.make_async_remote_copy(
            spec.at[me_q], spec.at[me_q], z_send.at[d], z_recv.at[me_q],
            device_id=(to_q * k + me_s, me_c), device_id_type=MESH,
        )
        copy.start()
        sends.append(copy)
    for d in range(1, cols_n):
        to_c = lax.rem(me_c + d, cols_n)
        copy = pltpu.make_async_remote_copy(
            spec.at[me_q], rowb.at[me_c], r_send.at[d], r_recv.at[me_c],
            device_id=(me_r, to_c), device_id_type=MESH,
        )
        copy.start()
        sends.append(copy)
    rowb[me_c] = spec[me_q]
    guarded = []
    for d in range(cols_n):
        q = lax.rem(me_q + d, cols_n)
        if d:
            pltpu.make_async_remote_copy(
                spec.at[q], spec.at[q], z_send.at[d], z_recv.at[q],
                device_id=(q * k + me_s, me_c), device_id_type=MESH,
            ).wait_recv()
        for e in range(k):
            copy = pltpu.make_async_remote_copy(
                spec.at[q], colb.at[me_s, me_c], c_send.at[d, e], c_recv.at[me_s, me_c],
                device_id=(me_q * k + lax.rem(me_s + e, k), q), device_id_type=MESH,
            )
            if e:
                copy.start()
                sends.append(copy)
            else:
                @pl.when(q != me_c)
                def _():
                    copy.start()

                @pl.when(q == me_c)
                def _():
                    colb[me_s, me_c] = spec[q]
                guarded.append((q, copy))

    for d in range(cols_n):
        c = lax.rem(me_c + d, cols_n)
        if d:
            pltpu.make_async_remote_copy(
                spec.at[me_q], rowb.at[c], r_send.at[d], r_recv.at[c],
                device_id=(me_r, c), device_id_type=MESH,
            ).wait_recv()
        for m in range(pm):
            rowf[:, d * pm + m, :] = rowb[c, m].astype(jnp.float32)
    for e in range(k):
        s = lax.rem(me_s + e, k)
        for d in range(cols_n):
            c = lax.rem(me_c + d, cols_n)
            if e or d:
                pltpu.make_async_remote_copy(
                    spec.at[me_q], colb.at[s, c], c_send.at[d, e], c_recv.at[s, c],
                    device_id=(me_q * k + s, c), device_id_type=MESH,
                ).wait_recv()
            for m in range(pm):
                colf[d * pm + m, pl.ds(pl.multiple_of(s * rc, rc), rc), :] = (
                    colb[s, c, m].astype(jnp.float32)
                )

    i_copy.wait()
    scale = jnp.float32(1.0 / minutes)
    step = 2

    def pair(p, carry):
        for v in range(nv):
            lo = v * LANES
            hi_ = F + v * LANES
            acc = [[None, None] for _ in range(step)]
            for m in range(minutes):
                cr = colf[m, :, lo:lo + LANES]
                ci = colf[m, :, hi_:hi_ + LANES]
                for u in range(step):
                    rr = rowf[p * step + u, m:m + 1, lo:lo + LANES]
                    ri = rowf[p * step + u, m:m + 1, hi_:hi_ + LANES]
                    real = rr * cr + ri * ci
                    imag = ri * cr - rr * ci
                    acc[u][0] = real if m == 0 else acc[u][0] + real
                    acc[u][1] = imag if m == 0 else acc[u][1] + imag
            for u in range(step):
                stacked[p * step + u, :, lo:lo + LANES] = (acc[u][0] * scale).astype(jnp.bfloat16)
                stacked[p * step + u, :, hi_:hi_ + LANES] = (acc[u][1] * scale).astype(jnp.bfloat16)
        return carry

    lax.fori_loop(0, rc // step, pair, 0)

    group = 256 // jc
    lags = out_ref.shape[2]

    def lagged(b, carry):
        left = stacked[pl.ds(b * group, group)].reshape(group * jc, 2 * F)
        result = jnp.dot(left, itab[...], preferred_element_type=jnp.float32)
        result = (result * jnp.float32(1.0 / math.sqrt(F))).astype(jnp.bfloat16)
        out_ref[pl.ds(b * group, group)] = result[:, :lags].reshape(group, jc, lags)
        return carry

    lax.fori_loop(0, rc // group, lagged, 0)

    for copy in sends:
        copy.wait_send()
    for q, copy in guarded:
        @pl.when(q != me_c)
        def _():
            copy.wait_send()


def body(rows_n, cols_n, records, channel_live, minute_valid):
    rc, pm, length = records.shape
    lags = 2 * MAXLAG + 1
    lag_pad = -(-lags // LANES) * LANES
    k = rows_n // cols_n
    minutes = pm * cols_n
    ftab = jnp.asarray(forward_table(length, F, length))
    itab = jnp.asarray(inverse_table(length, F, MAXLAG, lag_pad))
    jc = k * rc
    return pl.pallas_call(
        functools.partial(kernel, rows_n, cols_n, rc, pm),
        out_shape=jax.ShapeDtypeStruct((rc, jc, lags), jnp.bfloat16),
        in_specs=[
            pl.BlockSpec(memory_space=pltpu.SMEM),
            pl.BlockSpec(memory_space=pltpu.SMEM),
            pl.BlockSpec(memory_space=pltpu.VMEM),
            pl.BlockSpec(memory_space=pl.ANY),
            pl.BlockSpec(memory_space=pl.ANY),
        ],
        out_specs=pl.BlockSpec(memory_space=pltpu.VMEM),
        scratch_shapes=[
            pltpu.VMEM((length, 2 * F), jnp.bfloat16),
            pltpu.VMEM((2 * F, lag_pad), jnp.bfloat16),
            pltpu.VMEM((cols_n, pm, rc, 2 * F), jnp.bfloat16),
            pltpu.VMEM((cols_n, pm, rc, 2 * F), jnp.bfloat16),
            pltpu.VMEM((k, cols_n, pm, rc, 2 * F), jnp.bfloat16),
            pltpu.VMEM((rc, minutes, 2 * F), jnp.float32),
            pltpu.VMEM((minutes, jc, 2 * F), jnp.float32),
            pltpu.VMEM((rc, jc, 2 * F), jnp.bfloat16),
            pltpu.VMEM((2 * F // LANES, pm * rc, LANES), jnp.float32),
            pltpu.SemaphoreType.DMA((2,)),
            pltpu.SemaphoreType.DMA((cols_n,)),
            pltpu.SemaphoreType.DMA((cols_n,)),
            pltpu.SemaphoreType.DMA((cols_n,)),
            pltpu.SemaphoreType.DMA((cols_n,)),
            pltpu.SemaphoreType.DMA((cols_n, k)),
            pltpu.SemaphoreType.DMA((k, cols_n)),
        ],
        compiler_params=pltpu.CompilerParams(
            collective_id=0, has_side_effects=True, vmem_limit_bytes=56 * 1024 * 1024
        ),
    )(channel_live, minute_valid, records, ftab, itab)


def solution(mesh):
    in_specs = (P("row", "col", None), P(), P())
    out_specs = P("row", "col", None)
    run = functools.partial(body, mesh.shape["row"], mesh.shape["col"])
    return jax.shard_map(run, mesh=mesh, in_specs=in_specs, out_specs=out_specs, check_vma=False)
```

```python
import functools
import math

import jax
import jax.numpy as jnp
import numpy as np
from jax import lax
from jax.experimental import pallas as pl
from jax.experimental.pallas import tpu as pltpu
from jax.sharding import PartitionSpec as P

F = 640
BAND = 32
MAXLAG = 400
LANES = 128
MESH = pl.DeviceIdType.MESH


def forward_table(length, nfreq, padded):
    times = np.arange(length, dtype=np.int64)[:, None]
    freqs = np.arange(1, nfreq + 1, dtype=np.int64)[None, :]
    phase = (times * freqs % length).astype(np.float32) * np.float32(2.0 * math.pi / length)
    table = np.concatenate([np.cos(phase), -np.sin(phase)], axis=1)
    return np.pad(table, ((0, padded - length), (0, 0))).astype(jnp.bfloat16)


def inverse_table(length, nfreq, maxlag, padded):
    freqs = np.arange(1, nfreq + 1, dtype=np.int64)[:, None]
    shifts = np.arange(-maxlag, maxlag + 1, dtype=np.int64)[None, :]
    phase = np.mod(freqs * shifts, length).astype(np.float32) * np.float32(2.0 * math.pi / length)
    table = np.concatenate([np.cos(phase), -np.sin(phase)], axis=0)
    return np.pad(table, ((0, 0), (0, padded - table.shape[1]))).astype(jnp.bfloat16)


def kernel(
    rows_n, cols_n, rc, pm,
    live_ref, valid_ref, rec_ref, ftab_hbm, itab_hbm, out_ref,
    ftab, itab, spec, rowb, colb, rowf, colf, stacked, white,
    tab_sem, z_send, z_recv, r_send, r_recv, b_send, c_recv,
):
    k = rows_n // cols_n
    me_r = lax.axis_index("row")
    me_c = lax.axis_index("col")
    me_q = me_r // k
    me_s = lax.rem(me_r, k)
    minutes = pm * cols_n
    jc = k * rc

    f_copy = pltpu.make_async_copy(ftab_hbm, ftab, tab_sem.at[0])
    i_copy = pltpu.make_async_copy(itab_hbm, itab, tab_sem.at[1])
    f_copy.start()
    i_copy.start()

    def start_if(cond, copy, waits):
        if cond is None:
            copy.start()
        else:
            pl.when(cond)(copy.start)
        waits.append((cond, copy))

    above = me_q + 1 < cols_n
    below = me_q > 0
    up = jnp.minimum(me_q + 1, cols_n - 1) * k + me_s
    down = jnp.maximum(me_q - 1, 0) * k + me_s
    barrier = pltpu.get_barrier_semaphore()
    peers = []
    for e in range(k):
        for d in range(cols_n):
            if e or d:
                peers.append((me_q * k + lax.rem(me_s + e, k), lax.rem(me_c + d, cols_n)))
    for peer in peers:
        pl.semaphore_signal(barrier, inc=1, device_id=peer, device_id_type=MESH)

    @pl.when(above)
    def _():
        pl.semaphore_signal(barrier, inc=1, device_id=(up, me_c), device_id_type=MESH)

    @pl.when(below)
    def _():
        pl.semaphore_signal(barrier, inc=1, device_id=(down, me_c), device_id_type=MESH)

    f_copy.wait()
    raw = jnp.dot(rec_ref[...].reshape(pm * rc, rec_ref.shape[2]), ftab[...], preferred_element_type=jnp.float32)
    re = raw[:, :F]
    im = raw[:, F:]
    sq = re * re + im * im
    nv = F // LANES
    n = pm * rc
    sq = jnp.concatenate([sq[:, v * LANES:(v + 1) * LANES] for v in range(nv)], axis=0)
    shift = int(math.log2(BAND))
    same = (lax.broadcasted_iota(jnp.int32, (LANES, LANES), 0) >> shift) == (
        lax.broadcasted_iota(jnp.int32, (LANES, LANES), 1) >> shift
    )
    ones = jnp.where(same, 1.0, 0.0).astype(jnp.bfloat16)
    hi = sq.astype(jnp.bfloat16)
    rest = sq - hi.astype(jnp.float32)
    mid = rest.astype(jnp.bfloat16)
    low = (rest - mid.astype(jnp.float32)).astype(jnp.bfloat16)
    power = (
        jnp.dot(hi, ones, preferred_element_type=jnp.float32)
        + jnp.dot(mid, ones, preferred_element_type=jnp.float32)
        + jnp.dot(low, ones, preferred_element_type=jnp.float32)
    ) * jnp.float32(1.0 / (2 * BAND))
    weight = lax.rsqrt(power + 1e-06)
    weight = jnp.concatenate([weight[v * n:(v + 1) * n] for v in range(nv)], axis=1)
    row_at = lax.broadcasted_iota(jnp.int32, (rc, 1), 0)
    live = jnp.zeros((rc, 1), jnp.int32)
    for i in range(rc):
        live = jnp.where(row_at == i, live_ref[me_r * rc + i], live)
    live = live.astype(jnp.float32)
    for v in range(nv):
        at = slice(v * LANES, (v + 1) * LANES)
        white[v] = re[:, at] * weight[:, at]
        white[nv + v] = im[:, at] * weight[:, at]
    for m in range(pm):
        keep = live * valid_ref[me_c * pm + m].astype(jnp.float32)
        for v in range(2 * nv):
            spec[me_q, m, :, v * LANES:(v + 1) * LANES] = (
                white[v, pl.ds(m, rc, stride=pm), :] * keep
            ).astype(jnp.bfloat16)

    pl.semaphore_wait(
        barrier, len(peers) + above.astype(jnp.int32) + below.astype(jnp.int32)
    )

    def remote(src, dst, send, recv, device):
        return pltpu.make_async_remote_copy(
            src, dst, send, recv, device_id=device, device_id_type=MESH
        )

    waits = []
    parts = 2
    size = pm // parts

    def cut(part):
        return pl.ds(part * size, size)

    def hop(q, way, part):
        return remote(
            spec.at[q, cut(part)], spec.at[q, cut(part)], z_send.at[q, way, part], z_recv.at[q, part],
            (down if way else up, me_c),
        )

    def to_block(q, cond, part):
        other = q != me_c
        if cond is not None:
            other = jnp.logical_and(cond, other)
        for e in range(k):
            start_if(
                cond if e else other,
                remote(
                    spec.at[q, cut(part)], colb.at[me_s, me_c, cut(part)],
                    b_send.at[q, e, part], c_recv.at[me_s, me_c, part],
                    (me_q * k + lax.rem(me_s + e, k), q),
                ),
                waits,
            )

    for part in range(parts):
        start_if(above, hop(me_q, 0, part), waits)
        start_if(below, hop(me_q, 1, part), waits)
        to_block(me_q, None, part)
    for d in range(1, cols_n):
        start_if(
            None,
            remote(
                spec.at[me_q], rowb.at[me_c], r_send.at[d], r_recv.at[me_c],
                (me_r, lax.rem(me_c + d, cols_n)),
            ),
            waits,
        )
    rowb[me_c] = spec[me_q]
    for d in range(1, cols_n):
        low_ok = me_q >= d
        low_q = jnp.maximum(me_q - d, 0)
        high_ok = me_q + d < cols_n
        high_q = jnp.minimum(me_q + d, cols_n - 1)
        for part in range(parts):
            pl.when(low_ok)(hop(low_q, 0, part).wait_recv)
            start_if(jnp.logical_and(low_ok, above), hop(low_q, 0, part), waits)
            to_block(low_q, low_ok, part)
            pl.when(high_ok)(hop(high_q, 1, part).wait_recv)
            start_if(jnp.logical_and(high_ok, below), hop(high_q, 1, part), waits)
            to_block(high_q, high_ok, part)
    colb[me_s, me_c] = spec[me_c]

    for d in range(cols_n):
        c = lax.rem(me_c + d, cols_n)
        if d:
            remote(
                spec.at[me_q], rowb.at[c], r_send.at[d], r_recv.at[c], (me_r, c)
            ).wait_recv()
        for m in range(pm):
            rowf[:, d * pm + m, :] = rowb[c, m].astype(jnp.float32)
    for e in range(k):
        s = lax.rem(me_s + e, k)
        for d in range(cols_n):
            c = lax.rem(me_c + d, cols_n)
            if e or d:
                for part in range(parts):
                    remote(
                        spec.at[me_q, cut(part)], colb.at[s, c, cut(part)],
                        b_send.at[me_q, e, part], c_recv.at[s, c, part], (me_q * k + s, c),
                    ).wait_recv()
            for m in range(pm):
                colf[d * pm + m, pl.ds(pl.multiple_of(s * rc, rc), rc), :] = (
                    colb[s, c, m].astype(jnp.float32)
                )

    i_copy.wait()
    scale = jnp.float32(1.0 / minutes)
    step = 2

    def pair(p, carry):
        for v in range(nv):
            lo = v * LANES
            hi_ = F + v * LANES
            acc = [[None, None] for _ in range(step)]
            for m in range(minutes):
                cr = colf[m, :, lo:lo + LANES]
                ci = colf[m, :, hi_:hi_ + LANES]
                for u in range(step):
                    rr = rowf[p * step + u, m:m + 1, lo:lo + LANES]
                    ri = rowf[p * step + u, m:m + 1, hi_:hi_ + LANES]
                    real = rr * cr + ri * ci
                    imag = ri * cr - rr * ci
                    acc[u][0] = real if m == 0 else acc[u][0] + real
                    acc[u][1] = imag if m == 0 else acc[u][1] + imag
            for u in range(step):
                stacked[p * step + u, :, lo:lo + LANES] = (acc[u][0] * scale).astype(jnp.bfloat16)
                stacked[p * step + u, :, hi_:hi_ + LANES] = (acc[u][1] * scale).astype(jnp.bfloat16)
        return carry

    lax.fori_loop(0, rc // step, pair, 0)

    group = 256 // jc
    lags = out_ref.shape[2]

    def lagged(b, carry):
        left = stacked[pl.ds(b * group, group)].reshape(group * jc, 2 * F)
        result = jnp.dot(left, itab[...], preferred_element_type=jnp.float32)
        result = (result * jnp.float32(1.0 / math.sqrt(F))).astype(jnp.bfloat16)
        out_ref[pl.ds(b * group, group)] = result[:, :lags].reshape(group, jc, lags)
        return carry

    lax.fori_loop(0, rc // group, lagged, 0)

    for cond, copy in waits:
        if cond is None:
            copy.wait_send()
        else:
            pl.when(cond)(copy.wait_send)


def body(rows_n, cols_n, records, channel_live, minute_valid):
    rc, pm, length = records.shape
    lags = 2 * MAXLAG + 1
    lag_pad = -(-lags // LANES) * LANES
    k = rows_n // cols_n
    minutes = pm * cols_n
    ftab = jnp.asarray(forward_table(length, F, length))
    itab = jnp.asarray(inverse_table(length, F, MAXLAG, lag_pad))
    jc = k * rc
    return pl.pallas_call(
        functools.partial(kernel, rows_n, cols_n, rc, pm),
        out_shape=jax.ShapeDtypeStruct((rc, jc, lags), jnp.bfloat16),
        in_specs=[
            pl.BlockSpec(memory_space=pltpu.SMEM),
            pl.BlockSpec(memory_space=pltpu.SMEM),
            pl.BlockSpec(memory_space=pltpu.VMEM),
            pl.BlockSpec(memory_space=pl.ANY),
            pl.BlockSpec(memory_space=pl.ANY),
        ],
        out_specs=pl.BlockSpec(memory_space=pltpu.VMEM),
        scratch_shapes=[
            pltpu.VMEM((length, 2 * F), jnp.bfloat16),
            pltpu.VMEM((2 * F, lag_pad), jnp.bfloat16),
            pltpu.VMEM((cols_n, pm, rc, 2 * F), jnp.bfloat16),
            pltpu.VMEM((cols_n, pm, rc, 2 * F), jnp.bfloat16),
            pltpu.VMEM((k, cols_n, pm, rc, 2 * F), jnp.bfloat16),
            pltpu.VMEM((rc, minutes, 2 * F), jnp.float32),
            pltpu.VMEM((minutes, jc, 2 * F), jnp.float32),
            pltpu.VMEM((rc, jc, 2 * F), jnp.bfloat16),
            pltpu.VMEM((2 * F // LANES, pm * rc, LANES), jnp.float32),
            pltpu.SemaphoreType.DMA((2,)),
            pltpu.SemaphoreType.DMA((cols_n, 2, 2)),
            pltpu.SemaphoreType.DMA((cols_n, 2)),
            pltpu.SemaphoreType.DMA((cols_n,)),
            pltpu.SemaphoreType.DMA((cols_n,)),
            pltpu.SemaphoreType.DMA((cols_n, k, 2)),
            pltpu.SemaphoreType.DMA((k, cols_n, 2)),
        ],
        compiler_params=pltpu.CompilerParams(
            collective_id=0, has_side_effects=True, vmem_limit_bytes=56 * 1024 * 1024
        ),
    )(channel_live, minute_valid, records, ftab, itab)


def solution(mesh):
    in_specs = (P("row", "col", None), P(), P())
    out_specs = P("row", "col", None)
    run = functools.partial(body, mesh.shape["row"], mesh.shape["col"])
    return jax.shard_map(run, mesh=mesh, in_specs=in_specs, out_specs=out_specs, check_vma=False)
```
